256 devices in a mesh: slab: 64 (over z, x, core), lvl: 4 (over y).
Axes of the slice: x: 4, y: 4, z: 8, core: 2. Of those that a mesh axis runs over, the one named last changes fastest.
Arguments:
- multipoles: bfloat16 [216, 524288], P(None, 'slab'), may hold values from -6 to 6
- fine_m2l: bfloat16 [16, 216, 216], P('lvl'), may hold values from -0.109375 to 0.109375
- m2m: bfloat16 [8, 216, 216], replicated, may hold values from -0.15625 to 0.15625
- coarse_m2l: bfloat16 [16, 216, 216], P('lvl'), may hold values from -0.109375 to 0.109375
- fine_source: int32 [16, 524288], P(None, 'slab'), may hold values from 0 to 12288
- ghost_index: int32 [2, 131072], replicated, may hold values from 0 to 8191
- ghost_count: int32 [2, 64], replicated, may hold values from 0 to 2048
- owner: int32 [65536, 1], P('slab'), may hold values from 0 to 63; in each aligned block of 1024 rows (0 to 1023, 1024 to 2047, ...) at most 32 rows name the same one
- coarse_source: int32 [16, 131072], P(None, 'slab'), may hold values from 0 to 2048
Outputs:
- fine_local: float32 [216, 524288], P(None, ('slab', 'lvl'))
- coarse_local: float32 [216, 131072], P(None, ('slab', 'lvl'))
The draws below stay inside these ranges and needn't reach their ends.
Inputs may be any that keep to these rules, and one draw needn't show every extreme that they name: Among the 1024 parents of one slab, no owner is named more than 32 times, a bound that some block reaches.
All inputs are finite; a program needn't handle non-finite values.
Results may differ from the reference program's by a relative error of at most 0.0029.
Values may be sent and summed in bfloat16 or wider, within the bound.
No kernel may reach another device: no remote copies, remote signals or barrier semaphores. Data moves between devices by JAX's collectives and lax.ppermute only.
A program may use at most 128 MiB of HBM per device.

```python
import math
import jax
import jax.numpy as jnp
import numpy as np
from jax import lax

C = 216
LEAF_DEV = 8192
OPS_F = 16
OPS_C = 16
GHOST = 2048
PAR_DEV = 1024
CAP = 32
SLOTS = 2048
LEAVES = 524288
PARENTS = 65536
GHOSTS = 131072
COARSE = 131072
N_SLAB = 64


def set_ends(array, key, low, top_value):
    extent = array.shape
    place = [jax.random.randint(jax.random.fold_in(key, axis), (), 0, extent[axis]) for axis in range(len(extent))]
    array = array.at[tuple(place)].set(low)
    longest = extent.index(max(extent))
    place[longest] = (place[longest] + 1) % extent[longest]
    return array.at[tuple(place)].set(top_value)


def block_levels(key, dims, cuts, least, high):
    def one(dim, blocks):
        heights = jax.random.uniform(jax.random.fold_in(jax.random.fold_in(key, 6), dim), (blocks,), jnp.float32, least / len(cuts), high / len(cuts))
        return jnp.repeat(jnp.exp(heights), dims[dim] // blocks).reshape((-1,) + (1,) * (len(dims) - dim - 1))

    loudness = one(*cuts[0])
    for cut in cuts[1:]:
        loudness = loudness * one(*cut)
    return loudness


def routed_block(rng, own, number, rows, amount, top, reach, skew):
    ranking = jax.random.permutation(rng, amount)
    packed, common = shares(amount, rows * top, reach, skew, True), shares(amount, rows * top, reach, skew, False)
    places = jnp.arange(amount)

    def named(lengths, offset_by):
        used = int((lengths > 0).sum())
        fixed = max(1, used // 4)
        passed = fixed + (places - fixed + offset_by * (used - fixed)) % max(1, amount - fixed)
        return jnp.zeros((amount,), jnp.int32).at[ranking[jnp.where(places < fixed, places, passed)]].set(jnp.asarray(lengths, jnp.int32))

    lengths = jnp.where(number % 4 == 0, named(packed, number // 4), named(common, number - number // 4 - 1))
    mixed = jax.random.permutation(jax.random.fold_in(own, 3), amount)
    source_of, receiver = mixed[0:amount // 2 * 2:2], mixed[1:amount // 2 * 2:2]
    margin = jnp.minimum(lengths[source_of] - 1, reach - lengths[receiver]) // 2
    margin = jnp.where((source_of == ranking[0]) | (receiver == ranking[0]) | (lengths[receiver] == 0), 0, jnp.maximum(margin, 0))
    passed = jax.random.randint(jax.random.fold_in(own, 4), (amount // 2,), 0, 1 << 20) % (margin + 1)
    lengths = lengths.at[source_of].add(-passed).at[receiver].add(passed)
    items = jnp.searchsorted(jnp.cumsum(lengths), jnp.arange(rows * top), side="right").astype(jnp.int32)
    table = items.reshape(top, rows).T
    table = table[jax.random.permutation(jax.random.fold_in(own, 1), rows)]
    offset_by = jax.random.randint(jax.random.fold_in(own, 2), (rows, 1), 0, top)
    return jnp.take_along_axis(table, (jnp.arange(top)[None, :] + offset_by) % top, axis=1)


def shares(count, total, bound, lean, full):
    portions = [(1 << 20) // math.isqrt(standing ** lean) + 1 for standing in range(1, count + 1)]
    largest = bound if full else min(bound, max(-(-total // count), total * portions[0] // sum(portions)))
    least = 1 if total - largest >= count - 1 else 0
    counts, rest = [largest] + [least] * (count - 1), total - largest - least * (count - 1)
    while rest > 0:
        candidates = [i for i in range(1, count) if counts[i] < largest] or [i for i in range(1, count) if counts[i] < bound]
        mass, budget = sum([portions[i] for i in candidates]), rest
        for i in candidates:
            addition = min(bound - counts[i], max(1, budget * portions[i] // mass), rest)
            counts[i] = counts[i] + addition
            rest = rest - addition
    return np.array(counts)


def noise(own_key, extent, deviation, reach, shards=(), held_as=jnp.bfloat16):
    factor_of = block_levels(own_key, extent, shards, -0.22, 0.18) if shards else 1.0
    entries = jax.random.normal(own_key, extent, jnp.float32) * deviation * factor_of
    return jnp.minimum(jnp.maximum(entries, -reach), reach).astype(held_as)


def setup_inputs(seed: int = 0) -> dict:
    key_of = jax.random.split(jax.random.key(seed), 10)
    multipoles = noise(key_of[0], (C, LEAVES), 1.0, 6.0, ((1, 64),))
    fine_m2l = noise(key_of[1], (OPS_F, C, C), (C * OPS_F) ** -0.5, 0.109375, ((0, 4),))
    m2m = noise(key_of[2], (8, C, C), (8 * C) ** -0.5, 0.15625)
    coarse_m2l = noise(key_of[3], (OPS_C, C, C), (C * OPS_C) ** -0.5, 0.109375, ((0, 4),))
    fine_source = set_ends(jax.random.randint(key_of[4], (OPS_F, LEAVES), 0, LEAF_DEV + 2 * GHOST + 1), jax.random.fold_in(key_of[4], 1), 0, LEAF_DEV + 2 * GHOST).astype(jnp.int32)
    ghost_index = set_ends(jax.random.randint(key_of[5], (2, GHOSTS), 0, LEAF_DEV), jax.random.fold_in(key_of[5], 1), 0, LEAF_DEV - 1).astype(jnp.int32)
    ghost_count = set_ends(jax.random.randint(key_of[6], (2, N_SLAB), 0, GHOST + 1), jax.random.fold_in(key_of[6], 1), 0, GHOST).astype(jnp.int32)
    owner_keys = jax.random.split(jax.random.fold_in(key_of[7], 1), PARENTS // PAR_DEV)
    owner_turns = jax.random.permutation(jax.random.fold_in(key_of[7], 3), PARENTS // PAR_DEV)
    owner = jax.vmap(lambda own, number: routed_block(jax.random.fold_in(key_of[7], 2), own, number, PAR_DEV, N_SLAB, 1, CAP, 2))(owner_keys, owner_turns).reshape((PARENTS, 1))
    coarse_source = set_ends(jax.random.randint(key_of[8], (OPS_C, COARSE), 0, SLOTS + 1), jax.random.fold_in(key_of[8], 1), 0, SLOTS).astype(jnp.int32)
    return dict(multipoles=multipoles, fine_m2l=fine_m2l, m2m=m2m, coarse_m2l=coarse_m2l, fine_source=fine_source, ghost_index=ghost_index, ghost_count=ghost_count, owner=owner, coarse_source=coarse_source)


def ghost_rows(multipoles, ghost_index, ghost_count, target, direction_row):
    present = (target >= 0) & (target < N_SLAB)
    sender = jnp.clip(target, 0, N_SLAB - 1).astype(jnp.int32)
    block = lax.dynamic_slice_in_dim(multipoles, (sender * LEAF_DEV).astype(jnp.int32), LEAF_DEV, 1)
    index_row = lax.dynamic_slice_in_dim(ghost_index[direction_row], (sender * GHOST).astype(jnp.int32), GHOST, 0)
    columns = jnp.take(block, index_row, axis=1)
    inside = (jnp.arange(GHOST, dtype=jnp.int32) < ghost_count[direction_row, sender]) & present
    return jnp.where(inside[None, :], columns, jnp.zeros_like(columns))


def translate(stack, sources, buffer, targets):
    def add_term(op_index, totals):
        picked = jnp.take(buffer, sources[op_index], axis=1)
        return totals + jnp.dot(stack[op_index], picked, preferred_element_type=jnp.float32)
    return lax.fori_loop(0, stack.shape[0], add_term, jnp.zeros((C, targets), jnp.float32))


def reference(multipoles, fine_m2l, m2m, coarse_m2l, fine_source, ghost_index, ghost_count, owner, coarse_source):
    empty_column = jnp.zeros((C, 1), jnp.bfloat16)

    def fine_block(sender):
        own = lax.dynamic_slice_in_dim(multipoles, (sender * LEAF_DEV).astype(jnp.int32), LEAF_DEV, 1)
        lower = ghost_rows(multipoles, ghost_index, ghost_count, sender - 1, 1)
        upper = ghost_rows(multipoles, ghost_index, ghost_count, sender + 1, 0)
        buffer = jnp.concatenate([own, lower, upper, empty_column], axis=1)
        sources = lax.dynamic_slice_in_dim(fine_source, (sender * LEAF_DEV).astype(jnp.int32), LEAF_DEV, 1)
        return translate(fine_m2l, sources, buffer, LEAF_DEV)

    fine_blocks = lax.map(fine_block, jnp.arange(N_SLAB, dtype=jnp.int32))
    fine_local = jnp.transpose(fine_blocks, (1, 0, 2)).reshape(C, LEAVES)

    children = multipoles.reshape(C, PARENTS, 8).astype(jnp.float32)
    parents = jnp.einsum('oij,jpo->ip', m2m.astype(jnp.float32), children, precision=lax.Precision.HIGHEST)
    parent_values = parents.astype(jnp.bfloat16)
    owner_blocks = owner.reshape(N_SLAB, PAR_DEV)
    matches = (owner_blocks[:, :, None] == jnp.arange(N_SLAB, dtype=jnp.int32)[None, None, :]).astype(jnp.int32)
    before = jnp.cumsum(matches, axis=1) - matches
    slot_rank = jnp.sum(before * matches, axis=2)
    column = owner_blocks * SLOTS + jnp.arange(N_SLAB, dtype=jnp.int32)[:, None] * CAP + slot_rank
    coarse_in = jnp.zeros((C, COARSE), jnp.bfloat16).at[:, column.reshape(-1)].set(parent_values)

    def coarse_block(owner_index):
        start = (owner_index * SLOTS).astype(jnp.int32)
        buffer = jnp.concatenate([lax.dynamic_slice_in_dim(coarse_in, start, SLOTS, 1), empty_column], axis=1)
        sources = lax.dynamic_slice_in_dim(coarse_source, start, SLOTS, 1)
        return translate(coarse_m2l, sources, buffer, SLOTS)

    coarse_blocks = lax.map(coarse_block, jnp.arange(N_SLAB, dtype=jnp.int32))
    coarse_local = jnp.transpose(coarse_blocks, (1, 0, 2)).reshape(C, COARSE)
    return fine_local, coarse_local
```

```python
import jax
import jax.numpy as jnp
from jax import lax
from jax.experimental import pallas as pl
from jax.experimental.pallas import tpu as pltpu
from jax.sharding import PartitionSpec as P

COEFFS = 216
LANES = 128
OPS = 16
TILE = 256
LEAVES = 8192
GHOST = 2048
PARENTS = 1024
SLOTS = 2048
TAIL = 16
BLOCK = 256
GROUP = 2048

ANY = pl.BlockSpec(memory_space=pl.ANY)
VMEM = pl.BlockSpec(memory_space=pltpu.VMEM)
SMEM = pl.BlockSpec(memory_space=pltpu.SMEM)


def contract_lanes(a, b):
    return lax.dot_general(a, b, (((1,), (1,)), ((), ())), preferred_element_type=jnp.float32)


def rows_body(picks, x, rows, sent, spread, stage, sem):
    r = lax.broadcasted_iota(jnp.int32, (2 * BLOCK, BLOCK), 0)
    c = lax.broadcasted_iota(jnp.int32, (2 * BLOCK, BLOCK), 1)
    for h in range(2):
        spread[h] = jnp.where(r == 2 * c + h, 1.0, 0.0).astype(jnp.bfloat16)
    flat = rows.reshape(2 * (LEAVES + TAIL), LANES)
    rows[pl.ds(LEAVES, TAIL)] = jnp.zeros((TAIL, 2, LANES), jnp.bfloat16)
    blocks = LEAVES // BLOCK

    def move(b):
        here = pl.ds(pl.multiple_of(b * 2 * BLOCK, 2 * BLOCK), 2 * BLOCK)
        return pltpu.make_async_copy(stage.at[here], flat.at[here], sem)

    @pl.loop(0, blocks)
    def _(b):
        cols = pl.ds(pl.multiple_of(b * BLOCK, BLOCK), BLOCK)
        low = contract_lanes(spread[0], x[0:LANES, cols])
        high = contract_lanes(spread[1], x[LANES:COEFFS, cols])
        high = jnp.concatenate([high, jnp.zeros((2 * BLOCK, 2 * LANES - COEFFS), jnp.float32)], axis=1)
        here = pl.ds(pl.multiple_of(b * 2 * BLOCK, 2 * BLOCK), 2 * BLOCK)
        stage[here] = (low + high).astype(jnp.bfloat16)

    whole = pltpu.make_async_copy(stage, flat.at[pl.ds(0, 2 * LEAVES)], sem)
    whole.start()
    whole.wait()
    for d in range(2):
        for g in range(GHOST):
            f = d * GHOST + g
            sent[d, g] = rows[picks[f // LANES, f % LANES]]


def leaf_rows(multipoles, picks):
    return pl.pallas_call(
        rows_body,
        name="leaf_rows",
        in_specs=[SMEM, VMEM],
        out_specs=[VMEM, VMEM],
        out_shape=[
            jax.ShapeDtypeStruct((LEAVES + TAIL, 2, LANES), jnp.bfloat16),
            jax.ShapeDtypeStruct((2, GHOST, 2, LANES), jnp.bfloat16),
        ],
        scratch_shapes=[
            pltpu.VMEM((2, 2 * BLOCK, BLOCK), jnp.bfloat16),
            pltpu.VMEM((2 * LEAVES, LANES), jnp.bfloat16),
            pltpu.SemaphoreType.DMA(()),
        ],
        compiler_params=pltpu.CompilerParams(vmem_limit_bytes=40 << 20),
        cost_estimate=pl.CostEstimate(flops=6_000_000_000, bytes_accessed=10 << 20, transcendentals=0),
    )(picks, multipoles)


def parents_body(place, x, w, out, children, pairs, stage, rows, sem):
    out[...] = jnp.zeros_like(out)
    per_block = BLOCK // 8
    r = lax.broadcasted_iota(jnp.int32, (BLOCK, BLOCK), 0)
    c = lax.broadcasted_iota(jnp.int32, (BLOCK, BLOCK), 1)
    octant_major = jnp.where(c == (r % per_block) * 8 + r // per_block, 1.0, 0.0).astype(jnp.bfloat16)
    per_group = GROUP // 8

    @pl.loop(0, LEAVES // GROUP)
    def _(s):
        for b in range(GROUP // BLOCK):
            cols = pl.ds(pl.multiple_of(s * GROUP + b * BLOCK, BLOCK), BLOCK)
            sorted_rows = contract_lanes(octant_major, x[:, cols]).astype(jnp.bfloat16)
            for o in range(8):
                children[o, b * per_block : (b + 1) * per_block] = sorted_rows[o * per_block : (o + 1) * per_block]
        total = jnp.dot(children[0], w[0], preferred_element_type=jnp.float32)
        for o in range(1, 8):
            total += jnp.dot(children[o], w[o], preferred_element_type=jnp.float32)
        pairs[pl.ds(0, per_group, 2), :] = total[:, :LANES]
        pairs[pl.ds(1, per_group, 2), :] = total[:, LANES:]
        here = pl.ds(pl.multiple_of(s * 2 * per_group, 2 * per_group), 2 * per_group)
        stage[here] = pairs[...].astype(jnp.bfloat16)

    move = pltpu.make_async_copy(stage, rows.reshape(2 * PARENTS, LANES), sem)
    move.start()
    move.wait()
    for p in range(PARENTS):
        out[place[p // LANES, p % LANES]] = rows[p]


def placed_parents(multipoles, weights, place):
    return pl.pallas_call(
        parents_body,
        name="placed_parents",
        in_specs=[SMEM, VMEM, VMEM],
        out_specs=VMEM,
        out_shape=jax.ShapeDtypeStruct((SLOTS, 2, LANES), jnp.bfloat16),
        scratch_shapes=[
            pltpu.VMEM((8, GROUP // 8, COEFFS), jnp.bfloat16),
            pltpu.VMEM((GROUP // 4, LANES), jnp.float32),
            pltpu.VMEM((2 * PARENTS, LANES), jnp.bfloat16),
            pltpu.VMEM((PARENTS, 2, LANES), jnp.bfloat16),
            pltpu.SemaphoreType.DMA(()),
        ],
        compiler_params=pltpu.CompilerParams(vmem_limit_bytes=40 << 20),
        cost_estimate=pl.CostEstimate(flops=4_000_000_000, bytes_accessed=6 << 20, transcendentals=0),
    )(place, multipoles, weights)


def translate(name, sources, weights, parts, slots, gflops):
    targets = sources.shape[1]
    tiles = targets // TILE
    n = len(parts)
    width = OPS * TILE // LANES
    src = sources.reshape(OPS, tiles, TILE).swapaxes(0, 1).reshape(tiles, width, LANES)

    def body(src_ref, w, *refs):
        part_refs = refs[:n]
        out = refs[n]
        buf, za, zb, zz, res, sa, sb, psem, isem, zsem = refs[n + 1 :]
        copies = [
            pltpu.make_async_copy(part_refs[k].at[pl.ds(first, rows)], buf.at[pl.ds(start, rows)], psem.at[k])
            for k, (_, start, first, rows) in enumerate(parts)
        ]
        for copy in copies:
            copy.start()

        def fetch(tile, dst, which):
            return pltpu.make_async_copy(src_ref.at[tile], dst, isem.at[which])

        fetch(0, sa, 0).start()
        fetch(1, sb, 1).start()
        for copy in copies:
            copy.wait()

        def gather(idx, z):
            for o in range(OPS):
                for u in range(TILE):
                    f = o * TILE + u
                    z[o, u] = buf[idx[f // LANES, f % LANES]]

        def multiply(z, tile):
            relaid = pltpu.make_async_copy(z.reshape(OPS, 2 * TILE, LANES), zz, zsem)
            relaid.start()
            relaid.wait()
            lhs = jnp.concatenate([zz[o] for o in range(OPS)], axis=1)
            for h in range(2):
                d = jnp.dot(lhs, w[:, h * 256 : (h + 1) * 256], preferred_element_type=jnp.float32)
                res[2 * h] = d[:, :LANES]
                res[2 * h + 1] = d[:, LANES:]
            cols = pl.ds(pl.multiple_of(tile * TILE, TILE), TILE)
            for c in range(2):
                total = res[c, pl.ds(0, TILE, 2), :] + res[2 + c, pl.ds(1, TILE, 2), :]
                rows = min(LANES, COEFFS - c * LANES)
                out[c * LANES : c * LANES + rows, cols] = total.T[:rows]

        @pl.loop(0, tiles // 2)
        def _(i):
            fetch(0, sa, 0).wait()
            gather(sa, za)
            multiply(za, 2 * i)

            @pl.when(i < tiles // 2 - 1)
            def _():
                fetch(2 * i + 2, sa, 0).start()

            fetch(0, sb, 1).wait()
            gather(sb, zb)
            multiply(zb, 2 * i + 1)

            @pl.when(i < tiles // 2 - 1)
            def _():
                fetch(2 * i + 3, sb, 1).start()

    return pl.pallas_call(
        body,
        name=name,
        in_specs=[ANY, VMEM] + [ANY] * n,
        out_specs=VMEM,
        out_shape=jax.ShapeDtypeStruct((COEFFS, targets), jnp.float32),
        scratch_shapes=[
            pltpu.VMEM((slots, 2, LANES), jnp.bfloat16),
            pltpu.VMEM((OPS, TILE, 2, LANES), jnp.bfloat16),
            pltpu.VMEM((OPS, TILE, 2, LANES), jnp.bfloat16),
            pltpu.VMEM((OPS, 2 * TILE, LANES), jnp.bfloat16),
            pltpu.VMEM((4, 2 * TILE, LANES), jnp.float32),
            pltpu.SMEM((width, LANES), jnp.int32),
            pltpu.SMEM((width, LANES), jnp.int32),
            pltpu.SemaphoreType.DMA((n,)),
            pltpu.SemaphoreType.DMA((2,)),
            pltpu.SemaphoreType.DMA(()),
        ],
        compiler_params=pltpu.CompilerParams(vmem_limit_bytes=40 << 20),
        cost_estimate=pl.CostEstimate(flops=gflops * 1_000_000_000, bytes_accessed=10 << 20, transcendentals=0),
    )(src, weights, *[p[0] for p in parts])


def gathered_weights(stack):
    count = stack.shape[0]
    wide = 2 * LANES - COEFFS
    by_source = jnp.pad(jnp.swapaxes(stack, 1, 2), ((0, 0), (0, wide), (0, wide)))
    packed = by_source.reshape(count, 2, LANES, 2 * LANES).transpose(0, 2, 1, 3).reshape(count * LANES, 4 * LANES)
    return lax.all_gather(packed, "lvl", axis=0, tiled=True)


def passed_along(block, axis, distance):
    devices = range(lax.axis_size(axis))
    route = [(i - distance, i) for i in devices if i - distance in devices]
    return lax.ppermute(block, axis, route)


def per_device(multipoles, fine_m2l, m2m, coarse_m2l, fine_source, ghost_index, ghost_count, owner, coarse_source):
    slab_count = lax.axis_size("slab")
    slab_here = lax.axis_index("slab")
    level_count = lax.axis_size("lvl")
    level_here = lax.axis_index("lvl")

    index_here = lax.dynamic_slice_in_dim(ghost_index, slab_here * GHOST, GHOST, 1)
    count_here = lax.dynamic_slice_in_dim(ghost_count, slab_here, 1, 1)
    inside = jnp.arange(GHOST, dtype=jnp.int32)[None, :] < count_here
    picks = jnp.where(inside, index_here, LEAVES).reshape(2 * GHOST // LANES, LANES)

    rows, sent = leaf_rows(multipoles, picks)
    upper = passed_along(sent[0], "slab", -1)
    lower = passed_along(sent[1], "slab", 1)

    owners = owner[:, 0]
    matches = (owners[:, None] == jnp.arange(slab_count, dtype=jnp.int32)[None, :]).astype(jnp.bfloat16)
    order = jnp.arange(PARENTS, dtype=jnp.int32)
    earlier = (order[None, :] < order[:, None]).astype(jnp.bfloat16)
    before = jnp.dot(earlier, matches, preferred_element_type=jnp.float32)
    rank = jnp.sum(before * matches.astype(jnp.float32), axis=1).astype(jnp.int32)
    capacity = SLOTS // slab_count
    place = (owners * capacity + rank).reshape(PARENTS // LANES, LANES)
    m2m_by_source = jnp.pad(jnp.swapaxes(m2m, 1, 2), ((0, 0), (0, 0), (0, 2 * LANES - COEFFS)))
    outgoing = placed_parents(multipoles, m2m_by_source, place)
    received = lax.all_to_all(
        outgoing.reshape(slab_count, capacity, 2, LANES), "slab", split_axis=0, concat_axis=0, tiled=True
    ).reshape(SLOTS, 2, LANES)

    fine_weights = gathered_weights(fine_m2l)
    coarse_weights = gathered_weights(coarse_m2l)

    quarter = LEAVES // level_count
    fine_targets = lax.dynamic_slice_in_dim(fine_source, level_here * quarter, quarter, 1)
    fine_local = translate(
        "fine",
        fine_targets,
        fine_weights,
        [
            (rows, 0, 0, LEAVES),
            (lower, LEAVES, 0, GHOST),
            (upper, LEAVES + GHOST, 0, GHOST),
            (rows, LEAVES + 2 * GHOST, LEAVES, TAIL),
        ],
        LEAVES + 2 * GHOST + TAIL,
        20,
    )
    coarse_quarter = SLOTS // level_count
    coarse_targets = lax.dynamic_slice_in_dim(coarse_source, level_here * coarse_quarter, coarse_quarter, 1)
    coarse_local = translate(
        "coarse",
        coarse_targets,
        coarse_weights,
        [(received, 0, 0, SLOTS), (rows, SLOTS, LEAVES, TAIL)],
        SLOTS + TAIL,
        6,
    )
    return (fine_local, coarse_local)


def solution(mesh):
    placed = (
        P(None, "slab"),
        P("lvl", None, None),
        P(),
        P("lvl", None, None),
        P(None, "slab"),
        P(),
        P(),
        P("slab", None),
        P(None, "slab"),
    )
    return jax.shard_map(
        per_device,
        mesh=mesh,
        in_specs=placed,
        out_specs=(P(None, ("slab", "lvl")), P(None, ("slab", "lvl"))),
        check_vma=False,
    )
```

```python
import jax
import jax.numpy as jnp
from jax import lax
from jax.experimental import pallas as pl
from jax.experimental.pallas import tpu as pltpu
from jax.sharding import PartitionSpec as P

COEFFS = 216
LANES = 128
OPS = 16
TILE = 512
LEAVES = 8192
GHOST = 2048
PARENTS = 1024
SLOTS = 2048
TAIL = 16
BLOCK = 256
GROUP = 2048
CHUNKS = 8

ANY = pl.BlockSpec(memory_space=pl.ANY)
VMEM = pl.BlockSpec(memory_space=pltpu.VMEM)
SMEM = pl.BlockSpec(memory_space=pltpu.SMEM)


def contract_lanes(a, b):
    return lax.dot_general(a, b, (((1,), (1,)), ((), ())), preferred_element_type=jnp.float32)


def rows_body(picks, x_hbm, rows_hbm, down, up, x, spread, stage, rows, sent, xsem, osem):
    chunk = LEAVES // CHUNKS
    loads = []
    for k in range(CHUNKS):
        part = (slice(None), pl.ds(k * chunk, chunk))
        loads.append(pltpu.make_async_copy(x_hbm.at[part], x.at[part], xsem.at[k]))
        loads[k].start()
    r = lax.broadcasted_iota(jnp.int32, (2 * LANES, 2 * LANES), 0)
    c = lax.broadcasted_iota(jnp.int32, (2 * LANES, 2 * LANES), 1)
    spread[...] = jnp.where(r == 2 * (c % LANES) + c // LANES, 1.0, 0.0).astype(jnp.bfloat16)
    rows[pl.ds(2 * LEAVES, 2 * TAIL)] = jnp.zeros((2 * TAIL, LANES), jnp.float32)
    empty = jnp.zeros((2 * LANES - COEFFS, LANES), jnp.bfloat16)

    keeps = []
    for k in range(CHUNKS):
        loads[k].wait()
        for b in range(k * chunk // BLOCK, (k + 1) * chunk // BLOCK):
            halves = []
            for start in (b * BLOCK, b * BLOCK + LANES):
                cols = slice(start, start + LANES)
                high = jnp.concatenate([x[LANES:COEFFS, cols], empty], axis=0)
                halves.append(jnp.concatenate([x[0:LANES, cols], high], axis=1))
            both = contract_lanes(spread[...], jnp.concatenate(halves, axis=0))
            for h in range(2):
                here = pl.ds((2 * b + h) * BLOCK, BLOCK)
                rows[here] = both[:, h * LANES : (h + 1) * LANES]
                stage[here] = both[:, h * LANES : (h + 1) * LANES].astype(jnp.bfloat16)
        here = pl.ds(k * 2 * chunk, 2 * chunk)
        keeps.append(pltpu.make_async_copy(stage.at[here], rows_hbm.at[here], osem.at[k]))
        keeps[k].start()

    for d, out in enumerate((down, up)):
        for g in range(GHOST):
            f = d * GHOST + g
            sent[g] = rows[pl.ds(picks[f // LANES, f % LANES], 2), :]
        out[...] = sent.reshape(2 * GHOST, LANES)[...].astype(jnp.bfloat16)
    for keep in keeps:
        keep.wait()


def leaf_rows(multipoles, picks):
    ghosts = jax.ShapeDtypeStruct((2 * GHOST, LANES), jnp.bfloat16)
    return pl.pallas_call(
        rows_body,
        name="leaf_rows",
        in_specs=[SMEM, ANY],
        out_specs=[ANY, VMEM, VMEM],
        out_shape=[jax.ShapeDtypeStruct((2 * LEAVES, LANES), jnp.bfloat16), ghosts, ghosts],
        scratch_shapes=[
            pltpu.VMEM((COEFFS, LEAVES), jnp.bfloat16),
            pltpu.VMEM((2 * LANES, 2 * LANES), jnp.bfloat16),
            pltpu.VMEM((2 * LEAVES, LANES), jnp.bfloat16),
            pltpu.VMEM((2 * (LEAVES + TAIL), LANES), jnp.float32),
            pltpu.VMEM((GHOST, 2, LANES), jnp.float32),
            pltpu.SemaphoreType.DMA((CHUNKS,)),
            pltpu.SemaphoreType.DMA((CHUNKS,)),
        ],
        compiler_params=pltpu.CompilerParams(vmem_limit_bytes=60 << 20),
        cost_estimate=pl.CostEstimate(flops=6_000_000_000, bytes_accessed=10 << 20, transcendentals=0),
    )(picks, multipoles)


def parents_body(place, x_hbm, w_hbm, out, x, w, children, rows, placed, xsem, wsem):
    groups = LEAVES // GROUP
    loads = []
    for k in range(groups):
        part = (slice(None), pl.ds(k * GROUP, GROUP))
        loads.append(pltpu.make_async_copy(x_hbm.at[part], x.at[part], xsem.at[k]))
        loads[k].start()
    weights = pltpu.make_async_copy(w_hbm, w, wsem)
    weights.start()
    placed[...] = jnp.zeros_like(placed)
    per_block = BLOCK // 8
    r = lax.broadcasted_iota(jnp.int32, (BLOCK, BLOCK), 0)
    c = lax.broadcasted_iota(jnp.int32, (BLOCK, BLOCK), 1)
    octant_major = jnp.where(c == (r % per_block) * 8 + r // per_block, 1.0, 0.0).astype(jnp.bfloat16)
    per_group = GROUP // 8
    empty = jnp.zeros((per_group, 2 * LANES - COEFFS), jnp.float32)

    for s in range(groups):
        loads[s].wait()
        for b in range(GROUP // BLOCK):
            start = s * GROUP + b * BLOCK
            sorted_rows = contract_lanes(octant_major, x[:, start : start + BLOCK]).astype(jnp.bfloat16)
            for o in range(8):
                children[o, b * per_block : (b + 1) * per_block] = sorted_rows[o * per_block : (o + 1) * per_block]
        if s == 0:
            weights.wait()
        total = contract_lanes(children[0], w[0])
        for o in range(1, 8):
            total += contract_lanes(children[o], w[o])
        first = s * 2 * per_group
        rows[pl.ds(first, per_group, 2), :] = total[:, :LANES]
        rows[pl.ds(first + 1, per_group, 2), :] = jnp.concatenate([total[:, LANES:], empty], axis=1)

    box = rows.reshape(PARENTS, 2, LANES)
    for p in range(PARENTS):
        placed[pl.ds(place[p // LANES, p % LANES], 2), :] = box[p]
    out[...] = placed[...].astype(jnp.bfloat16)


def placed_parents(multipoles, weights, place):
    return pl.pallas_call(
        parents_body,
        name="placed_parents",
        in_specs=[SMEM, ANY, ANY],
        out_specs=VMEM,
        out_shape=jax.ShapeDtypeStruct((2 * SLOTS, LANES), jnp.bfloat16),
        scratch_shapes=[
            pltpu.VMEM((COEFFS, LEAVES), jnp.bfloat16),
            pltpu.VMEM((8, COEFFS, COEFFS), jnp.bfloat16),
            pltpu.VMEM((8, GROUP // 8, COEFFS), jnp.bfloat16),
            pltpu.VMEM((2 * PARENTS, LANES), jnp.float32),
            pltpu.VMEM((2 * SLOTS, LANES), jnp.float32),
            pltpu.SemaphoreType.DMA((LEAVES // GROUP,)),
            pltpu.SemaphoreType.DMA(()),
        ],
        compiler_params=pltpu.CompilerParams(vmem_limit_bytes=60 << 20),
        cost_estimate=pl.CostEstimate(flops=4_000_000_000, bytes_accessed=6 << 20, transcendentals=0),
    )(place, multipoles, weights)


def translate(name, sources, which_core, weights, swapped, parts, gflops):
    targets = sources.shape[1]
    tiles = targets // TILE
    n = len(parts)
    width = OPS * TILE // LANES
    src = sources.reshape(OPS, tiles, TILE).swapaxes(0, 1).reshape(tiles * width, LANES)
    sizes = [p.shape[0] for p in parts]
    starts = [sum(sizes[:k]) for k in range(n)]
    slots = sum(sizes)
    piece = 2048
    pieces = [(k, at) for k in range(n) for at in range(0, sizes[k], piece)]

    def body(core, src_ref, *refs):
        here, mine, other = refs[0], refs[1:4], refs[4:7]
        refs = refs[7:]
        part_refs = refs[:n]
        out = refs[n]
        stage, buf, z, raw, w, psem, wsem = refs[n + 1 :]
        copies = []
        for j, (k, at) in enumerate(pieces):
            into = stage.at[pl.ds(starts[k] + at, piece)]
            copies.append(pltpu.make_async_copy(part_refs[k].at[pl.ds(at, piece)], into, psem.at[j]))

        pltpu.make_async_copy(here, raw.at[pl.ds(0, 4)], wsem.at[0]).start()
        for q in range(3):
            into = raw.at[pl.ds(4 * q + 4, 4)]

            @pl.when(core[0] != swapped)
            def _():
                pltpu.make_async_copy(mine[q], into, wsem.at[q + 1]).start()

            @pl.when(core[0] == swapped)
            def _():
                pltpu.make_async_copy(other[q], into, wsem.at[q + 1]).start()

        for copy in copies:
            copy.start()
        for q in range(4):
            pltpu.make_async_copy(here, raw.at[pl.ds(4 * q, 4)], wsem.at[q]).wait()
        r = lax.broadcasted_iota(jnp.int32, (2 * LANES, COEFFS), 0)
        c = lax.broadcasted_iota(jnp.int32, (2 * LANES, COEFFS), 1)
        unit = jnp.where(r == c, 1.0, 0.0).astype(jnp.bfloat16)
        for o in range(OPS):
            w[o * 2 * LANES : (o + 1) * 2 * LANES] = contract_lanes(unit, raw[o]).astype(jnp.bfloat16)

        buf[pl.ds(slots, 2 * TAIL)] = jnp.zeros((2 * TAIL, LANES), jnp.float32)
        for copy, (k, at) in zip(copies, pieces):
            copy.wait()
            now = pl.ds(starts[k] + at, piece)
            buf[now] = stage[now].astype(jnp.float32)

        @pl.loop(0, tiles)
        def _(tile):
            for o in range(OPS):
                for u in range(TILE):
                    f = o * TILE + u
                    slot = src_ref.at[:, pl.ds(f % LANES, 1)][tile * width + f // LANES, 0]
                    z[o, u] = buf[pl.ds(slot, 2), :]
            halves = []
            for o in range(OPS):
                box = z.at[o].reshape(2 * TILE, LANES)
                for h in range(2):
                    halves.append(box[pl.ds(h, TILE, 2), :].astype(jnp.bfloat16))
            total = jnp.dot(jnp.concatenate(halves, axis=1), w[...], preferred_element_type=jnp.float32)
            columns = pl.ds(pl.multiple_of(tile * TILE, TILE), TILE)
            out[:, columns] = total.T

    return pl.pallas_call(
        body,
        name=name,
        in_specs=[SMEM, SMEM] + [ANY] * (7 + n),
        out_specs=VMEM,
        out_shape=jax.ShapeDtypeStruct((COEFFS, targets), jnp.float32),
        scratch_shapes=[
            pltpu.VMEM((slots, LANES), jnp.bfloat16),
            pltpu.VMEM((slots + 2 * TAIL, LANES), jnp.float32),
            pltpu.VMEM((OPS, TILE, 2, LANES), jnp.float32),
            pltpu.VMEM((OPS, COEFFS, COEFFS), jnp.bfloat16),
            pltpu.VMEM((OPS * 2 * LANES, COEFFS), jnp.bfloat16),
            pltpu.SemaphoreType.DMA((len(pieces),)),
            pltpu.SemaphoreType.DMA((4,)),
        ],
        compiler_params=pltpu.CompilerParams(vmem_limit_bytes=60 << 20),
        cost_estimate=pl.CostEstimate(flops=gflops * 1_000_000_000, bytes_accessed=10 << 20, transcendentals=0),
    )(which_core, src, *weights, *parts)


def passed_along(block, axis, distance):
    devices = range(lax.axis_size(axis))
    route = [(i - distance, i) for i in devices if i - distance in devices]
    return lax.ppermute(block, axis, route)


def turned(block, distance):
    size = lax.axis_size("lvl")
    return lax.ppermute(block, "lvl", [((i + distance) % size, i) for i in range(size)])


def swapped_cores(block):
    return lax.ppermute(block, "slab", [(i ^ 1, i) for i in range(lax.axis_size("slab"))])


def sources_here(sources, level_here, level_count):
    quarter = sources.shape[1] // level_count
    here = 2 * lax.dynamic_slice_in_dim(sources, level_here * quarter, quarter, 1)
    return lax.dynamic_slice_in_dim(jnp.concatenate([here, here], axis=0), level_here * (OPS // level_count), OPS, 0)


def per_device(multipoles, fine_m2l, m2m, coarse_m2l, fine_source, ghost_index, ghost_count, owner, coarse_source):
    slab_count = lax.axis_size("slab")
    slab_here = lax.axis_index("slab")
    level_count = lax.axis_size("lvl")
    level_here = lax.axis_index("lvl")

    core = slab_here % 2
    fetched = jnp.where(core == 0, fine_m2l, coarse_m2l)
    mine = [turned(fetched, d) for d in (1, 2, 3)]
    other = [swapped_cores(m) for m in mine]
    core_flag = core.astype(jnp.int32).reshape(1)

    index_here = lax.dynamic_slice_in_dim(ghost_index, slab_here * GHOST, GHOST, 1)
    count_here = lax.dynamic_slice_in_dim(ghost_count, slab_here, 1, 1)
    inside = jnp.arange(GHOST, dtype=jnp.int32)[None, :] < count_here
    picks = jnp.where(inside, 2 * index_here, 2 * LEAVES).reshape(2 * GHOST // LANES, LANES)
    rows, down, up = leaf_rows(multipoles, picks)
    upper = passed_along(down, "slab", -1)
    lower = passed_along(up, "slab", 1)

    owners = owner[:, 0]
    matches = (owners[:, None] == jnp.arange(slab_count, dtype=jnp.int32)[None, :]).astype(jnp.bfloat16)
    order = jnp.arange(PARENTS, dtype=jnp.int32)
    earlier = (order[None, :] < order[:, None]).astype(jnp.bfloat16)
    before = jnp.dot(earlier, matches, preferred_element_type=jnp.float32)
    rank = jnp.sum(before * matches.astype(jnp.float32), axis=1).astype(jnp.int32)
    capacity = SLOTS // slab_count
    place = (2 * (owners * capacity + rank)).reshape(PARENTS // LANES, LANES)
    place, rows = lax.optimization_barrier((place, rows))
    outgoing = placed_parents(multipoles, m2m, place)
    received = lax.all_to_all(
        outgoing.reshape(slab_count, 2 * capacity, LANES), "slab", split_axis=0, concat_axis=0, tiled=True
    ).reshape(2 * SLOTS, LANES)

    fine_local = translate(
        "fine",
        sources_here(fine_source, level_here, level_count),
        core_flag,
        [fine_m2l, *mine, *other],
        1,
        [rows, lower, upper],
        20,
    )
    coarse_local = translate(
        "coarse",
        sources_here(coarse_source, level_here, level_count),
        core_flag,
        [coarse_m2l, *mine, *other],
        0,
        [received],
        6,
    )
    return (fine_local, coarse_local)


def solution(mesh):
    placed = (
        P(None, "slab"),
        P("lvl", None, None),
        P(),
        P("lvl", None, None),
        P(None, "slab"),
        P(),
        P(),
        P("slab", None),
        P(None, "slab"),
    )
    return jax.shard_map(
        per_device,
        mesh=mesh,
        in_specs=placed,
        out_specs=(P(None, ("slab", "lvl")), P(None, ("slab", "lvl"))),
        check_vma=False,
    )
```

```python
import jax
import jax.numpy as jnp
from jax import lax
from jax.experimental import pallas as pl
from jax.experimental.pallas import tpu as pltpu
from jax.sharding import PartitionSpec as P

COEFFS = 216
LANES = 128
OPS = 16
TILE = 512
LEAVES = 8192
GHOST = 2048
PARENTS = 1024
SLOTS = 2048
TAIL = 16
BLOCK = 256
GROUP = 2048
CHUNKS = 8

ANY = pl.BlockSpec(memory_space=pl.ANY)
VMEM = pl.BlockSpec(memory_space=pltpu.VMEM)
SMEM = pl.BlockSpec(memory_space=pltpu.SMEM)


def contract_lanes(a, b):
    return lax.dot_general(a, b, (((1,), (1,)), ((), ())), preferred_element_type=jnp.float32)


def spread_matrix():
    r = lax.broadcasted_iota(jnp.int32, (2 * LANES, 2 * LANES), 0)
    c = lax.broadcasted_iota(jnp.int32, (2 * LANES, 2 * LANES), 1)
    return jnp.where(r == 2 * (c % LANES) + c // LANES, 1.0, 0.0).astype(jnp.bfloat16)


def column_loads(x_hbm, x, sem):
    chunk = LEAVES // CHUNKS
    loads = []
    for k in range(CHUNKS):
        part = (slice(None), pl.ds(k * chunk, chunk))
        loads.append(pltpu.make_async_copy(x_hbm.at[part], x.at[part], sem.at[k]))
    return loads


def columns_to_rows(x, spread, rows, k):
    chunk = LEAVES // CHUNKS
    empty = jnp.zeros((2 * LANES - COEFFS, LANES), jnp.bfloat16)
    for b in range(k * chunk // BLOCK, (k + 1) * chunk // BLOCK):
        halves = []
        for start in (b * BLOCK, b * BLOCK + LANES):
            cols = slice(start, start + LANES)
            high = jnp.concatenate([x[LANES:COEFFS, cols], empty], axis=0)
            halves.append(jnp.concatenate([x[0:LANES, cols], high], axis=1))
        both = contract_lanes(spread[...], jnp.concatenate(halves, axis=0))
        for h in range(2):
            rows[pl.ds((2 * b + h) * BLOCK, BLOCK)] = both[:, h * LANES : (h + 1) * LANES]


def rows_body(picks, x_hbm, down, up, x, spread, rows, sent, xsem):
    loads = column_loads(x_hbm, x, xsem)
    for load in loads:
        load.start()
    spread[...] = spread_matrix()
    rows[pl.ds(2 * LEAVES, 2 * TAIL)] = jnp.zeros((2 * TAIL, LANES), jnp.float32)
    for k in range(CHUNKS):
        loads[k].wait()
        columns_to_rows(x, spread, rows, k)
    for d, out in enumerate((down, up)):
        for g in range(GHOST):
            f = d * GHOST + g
            sent[g] = rows[pl.ds(picks[f // LANES, f % LANES], 2), :]
        out[...] = sent.reshape(2 * GHOST, LANES)[...].astype(jnp.bfloat16)


def leaf_rows(multipoles, picks):
    ghosts = jax.ShapeDtypeStruct((2 * GHOST, LANES), jnp.bfloat16)
    return pl.pallas_call(
        rows_body,
        name="leaf_rows",
        in_specs=[SMEM, ANY],
        out_specs=[VMEM, VMEM],
        out_shape=[ghosts, ghosts],
        scratch_shapes=[
            pltpu.VMEM((COEFFS, LEAVES), jnp.bfloat16),
            pltpu.VMEM((2 * LANES, 2 * LANES), jnp.bfloat16),
            pltpu.VMEM((2 * (LEAVES + TAIL), LANES), jnp.float32),
            pltpu.VMEM((GHOST, 2, LANES), jnp.float32),
            pltpu.SemaphoreType.DMA((CHUNKS,)),
        ],
        compiler_params=pltpu.CompilerParams(vmem_limit_bytes=60 << 20),
        cost_estimate=pl.CostEstimate(flops=6_000_000_000, bytes_accessed=10 << 20, transcendentals=0),
    )(picks, multipoles)


def parents_body(place, x_hbm, w_hbm, out, x, w, children, rows, placed, xsem, wsem):
    groups = LEAVES // GROUP
    loads = []
    for k in range(groups):
        part = (slice(None), pl.ds(k * GROUP, GROUP))
        loads.append(pltpu.make_async_copy(x_hbm.at[part], x.at[part], xsem.at[k]))
    weights = pltpu.make_async_copy(w_hbm, w, wsem)
    loads[0].start()
    weights.start()
    for load in loads[1:]:
        load.start()
    placed[...] = jnp.zeros_like(placed)
    per_block = BLOCK // 8
    r = lax.broadcasted_iota(jnp.int32, (BLOCK, BLOCK), 0)
    c = lax.broadcasted_iota(jnp.int32, (BLOCK, BLOCK), 1)
    octant_major = jnp.where(c == (r % per_block) * 8 + r // per_block, 1.0, 0.0).astype(jnp.bfloat16)
    per_group = GROUP // 8
    empty = jnp.zeros((per_group, 2 * LANES - COEFFS), jnp.float32)

    for s in range(groups):
        loads[s].wait()
        for b in range(GROUP // BLOCK):
            start = s * GROUP + b * BLOCK
            sorted_rows = contract_lanes(octant_major, x[:, start : start + BLOCK]).astype(jnp.bfloat16)
            for o in range(8):
                children[o, b * per_block : (b + 1) * per_block] = sorted_rows[o * per_block : (o + 1) * per_block]
        if s == 0:
            weights.wait()
        total = contract_lanes(children[0], w[0])
        for o in range(1, 8):
            total += contract_lanes(children[o], w[o])
        first = s * 2 * per_group
        rows[pl.ds(first, per_group, 2), :] = total[:, :LANES]
        rows[pl.ds(first + 1, per_group, 2), :] = jnp.concatenate([total[:, LANES:], empty], axis=1)

    box = rows.reshape(PARENTS, 2, LANES)
    for p in range(PARENTS):
        placed[pl.ds(place[p // LANES, p % LANES], 2), :] = box[p]
    out[...] = placed[...].astype(jnp.bfloat16)


def placed_parents(multipoles, weights, place):
    return pl.pallas_call(
        parents_body,
        name="placed_parents",
        in_specs=[SMEM, ANY, ANY],
        out_specs=VMEM,
        out_shape=jax.ShapeDtypeStruct((2 * SLOTS, LANES), jnp.bfloat16),
        scratch_shapes=[
            pltpu.VMEM((COEFFS, LEAVES), jnp.bfloat16),
            pltpu.VMEM((8, COEFFS, COEFFS), jnp.bfloat16),
            pltpu.VMEM((8, GROUP // 8, COEFFS), jnp.bfloat16),
            pltpu.VMEM((2 * PARENTS, LANES), jnp.float32),
            pltpu.VMEM((2 * SLOTS, LANES), jnp.float32),
            pltpu.SemaphoreType.DMA((LEAVES // GROUP,)),
            pltpu.SemaphoreType.DMA(()),
        ],
        compiler_params=pltpu.CompilerParams(vmem_limit_bytes=60 << 20),
        cost_estimate=pl.CostEstimate(flops=4_000_000_000, bytes_accessed=6 << 20, transcendentals=0),
    )(place, multipoles, weights)


def translate(name, sources, which_core, weights, swapped, multipoles, parts, gflops):
    targets = sources.shape[1]
    tiles = targets // TILE
    n = len(parts)
    width = OPS * TILE // LANES
    src = sources.reshape(OPS, tiles, TILE).swapaxes(0, 1).reshape(tiles * width, LANES)
    leaves = [] if multipoles is None else [multipoles]
    starts = [2 * LEAVES * len(leaves)]
    for p in parts:
        starts.append(starts[-1] + p.shape[0])
    slots = starts[-1]

    def body(core, src_ref, *refs):
        here, mine, other = refs[0], refs[1:4], refs[4:7]
        refs = refs[7:]
        part_refs = refs[:n]
        refs = refs[n:]
        x_hbm = refs[: len(leaves)]
        refs = refs[len(leaves) :]
        out, buf, z, raw, w, wsem = refs[:6]
        loads = []
        if leaves:
            x, spread, xsem = refs[6:]
            loads = column_loads(x_hbm[0], x, xsem)
            for load in loads:
                load.start()

        pltpu.make_async_copy(here, raw.at[pl.ds(0, 4)], wsem.at[0]).start()
        for q in range(3):
            into = raw.at[pl.ds(4 * q + 4, 4)]

            @pl.when(core[0] != swapped)
            def _():
                pltpu.make_async_copy(mine[q], into, wsem.at[q + 1]).start()

            @pl.when(core[0] == swapped)
            def _():
                pltpu.make_async_copy(other[q], into, wsem.at[q + 1]).start()

        buf[pl.ds(slots, 2 * TAIL)] = jnp.zeros((2 * TAIL, LANES), jnp.float32)
        for k in range(n):
            buf[pl.ds(starts[k], starts[k + 1] - starts[k])] = part_refs[k][...].astype(jnp.float32)
        if leaves:
            spread[...] = spread_matrix()
            for k in range(CHUNKS):
                loads[k].wait()
                columns_to_rows(x, spread, buf, k)
        for q in range(4):
            pltpu.make_async_copy(here, raw.at[pl.ds(4 * q, 4)], wsem.at[q]).wait()
        r = lax.broadcasted_iota(jnp.int32, (2 * LANES, COEFFS), 0)
        c = lax.broadcasted_iota(jnp.int32, (2 * LANES, COEFFS), 1)
        unit = jnp.where(r == c, 1.0, 0.0).astype(jnp.bfloat16)
        for o in range(OPS):
            w[o * 2 * LANES : (o + 1) * 2 * LANES] = contract_lanes(unit, raw[o]).astype(jnp.bfloat16)

        @pl.loop(0, tiles)
        def _(tile):
            for o in range(OPS):
                for u in range(TILE):
                    f = o * TILE + u
                    slot = src_ref.at[:, pl.ds(f % LANES, 1)][tile * width + f // LANES, 0]
                    z[o, u] = buf[pl.ds(slot, 2), :]
            halves = []
            for o in range(OPS):
                box = z.at[o].reshape(2 * TILE, LANES)
                for h in range(2):
                    halves.append(box[pl.ds(h, TILE, 2), :].astype(jnp.bfloat16))
            total = jnp.dot(jnp.concatenate(halves, axis=1), w[...], preferred_element_type=jnp.float32)
            columns = pl.ds(pl.multiple_of(tile * TILE, TILE), TILE)
            out[:, columns] = total.T

    return pl.pallas_call(
        body,
        name=name,
        in_specs=[SMEM, SMEM] + [ANY] * 7 + [VMEM] * n + [ANY] * len(leaves),
        out_specs=VMEM,
        out_shape=jax.ShapeDtypeStruct((COEFFS, targets), jnp.float32),
        scratch_shapes=[
            pltpu.VMEM((slots + 2 * TAIL, LANES), jnp.float32),
            pltpu.VMEM((OPS, TILE, 2, LANES), jnp.float32),
            pltpu.VMEM((OPS, COEFFS, COEFFS), jnp.bfloat16),
            pltpu.VMEM((OPS * 2 * LANES, COEFFS), jnp.bfloat16),
            pltpu.SemaphoreType.DMA((4,)),
        ]
        + [
            pltpu.VMEM((COEFFS, LEAVES), jnp.bfloat16),
            pltpu.VMEM((2 * LANES, 2 * LANES), jnp.bfloat16),
            pltpu.SemaphoreType.DMA((CHUNKS,)),
        ]
        * len(leaves),
        compiler_params=pltpu.CompilerParams(vmem_limit_bytes=60 << 20),
        cost_estimate=pl.CostEstimate(flops=gflops * 1_000_000_000, bytes_accessed=10 << 20, transcendentals=0),
    )(which_core, src, *weights, *parts, *leaves)


def passed_along(block, axis, distance):
    devices = range(lax.axis_size(axis))
    route = [(i - distance, i) for i in devices if i - distance in devices]
    return lax.ppermute(block, axis, route)


def turned(block, distance):
    size = lax.axis_size("lvl")
    return lax.ppermute(block, "lvl", [((i + distance) % size, i) for i in range(size)])


def swapped_cores(block):
    return lax.ppermute(block, "slab", [(i ^ 1, i) for i in range(lax.axis_size("slab"))])


def sources_here(sources, level_here, level_count):
    quarter = sources.shape[1] // level_count
    here = 2 * lax.dynamic_slice_in_dim(sources, level_here * quarter, quarter, 1)
    return lax.dynamic_slice_in_dim(jnp.concatenate([here, here], axis=0), level_here * (OPS // level_count), OPS, 0)


def per_device(multipoles, fine_m2l, m2m, coarse_m2l, fine_source, ghost_index, ghost_count, owner, coarse_source):
    slab_count = lax.axis_size("slab")
    slab_here = lax.axis_index("slab")
    level_count = lax.axis_size("lvl")
    level_here = lax.axis_index("lvl")

    core = slab_here % 2
    fetched = jnp.where(core == 0, fine_m2l, coarse_m2l)
    mine = [turned(fetched, d) for d in (1, 2, 3)]
    other = [swapped_cores(m) for m in mine]
    core_flag = core.astype(jnp.int32).reshape(1)

    index_here = lax.dynamic_slice_in_dim(ghost_index, slab_here * GHOST, GHOST, 1)
    count_here = lax.dynamic_slice_in_dim(ghost_count, slab_here, 1, 1)
    inside = jnp.arange(GHOST, dtype=jnp.int32)[None, :] < count_here
    picks = jnp.where(inside, 2 * index_here, 2 * LEAVES).reshape(2 * GHOST // LANES, LANES)
    down, up = leaf_rows(multipoles, picks)
    upper = passed_along(down, "slab", -1)
    lower = passed_along(up, "slab", 1)

    owners = owner[:, 0]
    matches = (owners[:, None] == jnp.arange(slab_count, dtype=jnp.int32)[None, :]).astype(jnp.bfloat16)
    order = jnp.arange(PARENTS, dtype=jnp.int32)
    earlier = (order[None, :] < order[:, None]).astype(jnp.bfloat16)
    before = jnp.dot(earlier, matches, preferred_element_type=jnp.float32)
    rank = jnp.sum(before * matches.astype(jnp.float32), axis=1).astype(jnp.int32)
    capacity = SLOTS // slab_count
    place = (2 * (owners * capacity + rank)).reshape(PARENTS // LANES, LANES)
    place, down = lax.optimization_barrier((place, down))
    outgoing = placed_parents(multipoles, m2m, place)
    received = lax.all_to_all(
        outgoing.reshape(slab_count, 2 * capacity, LANES), "slab", split_axis=0, concat_axis=0, tiled=True
    ).reshape(2 * SLOTS, LANES)

    fine_local = translate(
        "fine",
        sources_here(fine_source, level_here, level_count),
        core_flag,
        [fine_m2l, *mine, *other],
        1,
        multipoles,
        [lower, upper],
        20,
    )
    coarse_local = translate(
        "coarse",
        sources_here(coarse_source, level_here, level_count),
        core_flag,
        [coarse_m2l, *mine, *other],
        0,
        None,
        [received],
        6,
    )
    return (fine_local, coarse_local)


def solution(mesh):
    placed = (
        P(None, "slab"),
        P("lvl", None, None),
        P(),
        P("lvl", None, None),
        P(None, "slab"),
        P(),
        P(),
        P("slab", None),
        P(None, "slab"),
    )
    return jax.shard_map(
        per_device,
        mesh=mesh,
        in_specs=placed,
        out_specs=(P(None, ("slab", "lvl")), P(None, ("slab", "lvl"))),
        check_vma=False,
    )
```

```python
import jax
import jax.numpy as jnp
from jax import lax
from jax.experimental import pallas as pl
from jax.experimental.pallas import tpu as pltpu
from jax.sharding import PartitionSpec as P

COEFFS = 216
LANES = 128
OPS = 16
TILE = 512
LEAVES = 8192
GHOST = 2048
PARENTS = 1024
SLOTS = 2048
TAIL = 16
BLOCK = 256
GROUP = 2048
CHUNKS = 8

ANY = pl.BlockSpec(memory_space=pl.ANY)
VMEM = pl.BlockSpec(memory_space=pltpu.VMEM)
SMEM = pl.BlockSpec(memory_space=pltpu.SMEM)


def contract_lanes(a, b):
    return lax.dot_general(a, b, (((1,), (1,)), ((), ())), preferred_element_type=jnp.float32)


def spread_matrix():
    r = lax.broadcasted_iota(jnp.int32, (2 * LANES, 2 * LANES), 0)
    c = lax.broadcasted_iota(jnp.int32, (2 * LANES, 2 * LANES), 1)
    return jnp.where(r == 2 * (c % LANES) + c // LANES, 1.0, 0.0).astype(jnp.bfloat16)


def column_loads(x_hbm, x, sem):
    chunk = LEAVES // CHUNKS
    loads = []
    for k in range(CHUNKS):
        part = (slice(None), pl.ds(k * chunk, chunk))
        loads.append(pltpu.make_async_copy(x_hbm.at[part], x.at[part], sem.at[k]))
    return loads


def columns_to_rows(x, spread, rows, k):
    chunk = LEAVES // CHUNKS
    empty = jnp.zeros((2 * LANES - COEFFS, LANES), jnp.bfloat16)
    for b in range(k * chunk // BLOCK, (k + 1) * chunk // BLOCK):
        halves = []
        for start in (b * BLOCK, b * BLOCK + LANES):
            cols = slice(start, start + LANES)
            high = jnp.concatenate([x[LANES:COEFFS, cols], empty], axis=0)
            halves.append(jnp.concatenate([x[0:LANES, cols], high], axis=1))
        both = contract_lanes(spread[...], jnp.concatenate(halves, axis=0))
        for h in range(2):
            rows[pl.ds((2 * b + h) * BLOCK, BLOCK)] = both[:, h * LANES : (h + 1) * LANES]


def upward_body(picks, place, x_hbm, w_hbm, down, up, out, *scratch):
    x, spread, rows, sent, w, children, boxes, placed, xsem, wsem = scratch
    loads = column_loads(x_hbm, x, xsem)
    weights = pltpu.make_async_copy(w_hbm, w, wsem)
    for load in loads[:4]:
        load.start()
    weights.start()
    for load in loads[4:]:
        load.start()
    spread[...] = spread_matrix()
    rows[pl.ds(2 * LEAVES, 2 * TAIL)] = jnp.zeros((2 * TAIL, LANES), jnp.float32)
    placed[...] = jnp.zeros_like(placed)
    per_block = BLOCK // 8
    r = lax.broadcasted_iota(jnp.int32, (BLOCK, BLOCK), 0)
    c = lax.broadcasted_iota(jnp.int32, (BLOCK, BLOCK), 1)
    octant_major = jnp.where(c == (r % per_block) * 8 + r // per_block, 1.0, 0.0).astype(jnp.bfloat16)
    per_group = GROUP // 8
    empty = jnp.zeros((per_group, 2 * LANES - COEFFS), jnp.float32)
    chunks = CHUNKS * GROUP // LEAVES

    for s in range(LEAVES // GROUP):
        for k in range(s * chunks, (s + 1) * chunks):
            loads[k].wait()
            columns_to_rows(x, spread, rows, k)
        for b in range(GROUP // BLOCK):
            start = s * GROUP + b * BLOCK
            sorted_rows = contract_lanes(octant_major, x[:, start : start + BLOCK]).astype(jnp.bfloat16)
            for o in range(8):
                children[o, b * per_block : (b + 1) * per_block] = sorted_rows[o * per_block : (o + 1) * per_block]
        if s == 0:
            weights.wait()
        total = contract_lanes(children[0], w[0])
        for o in range(1, 8):
            total += contract_lanes(children[o], w[o])
        first = s * 2 * per_group
        boxes[pl.ds(first, per_group, 2), :] = total[:, :LANES]
        boxes[pl.ds(first + 1, per_group, 2), :] = jnp.concatenate([total[:, LANES:], empty], axis=1)

    for d, ghosts in enumerate((down, up)):
        for g in range(GHOST):
            f = d * GHOST + g
            sent[g] = rows[pl.ds(picks[f // LANES, f % LANES], 2), :]
        ghosts[...] = sent.reshape(2 * GHOST, LANES)[...].astype(jnp.bfloat16)
    box = boxes.reshape(PARENTS, 2, LANES)
    for p in range(PARENTS):
        placed[pl.ds(place[p // LANES, p % LANES], 2), :] = box[p]
    out[...] = placed[...].astype(jnp.bfloat16)


def upward(multipoles, m2m, picks, place):
    ghosts = jax.ShapeDtypeStruct((2 * GHOST, LANES), jnp.bfloat16)
    return pl.pallas_call(
        upward_body,
        name="upward",
        in_specs=[SMEM, SMEM, ANY, ANY],
        out_specs=[VMEM, VMEM, VMEM],
        out_shape=[ghosts, ghosts, jax.ShapeDtypeStruct((2 * SLOTS, LANES), jnp.bfloat16)],
        scratch_shapes=[
            pltpu.VMEM((COEFFS, LEAVES), jnp.bfloat16),
            pltpu.VMEM((2 * LANES, 2 * LANES), jnp.bfloat16),
            pltpu.VMEM((2 * (LEAVES + TAIL), LANES), jnp.float32),
            pltpu.VMEM((GHOST, 2, LANES), jnp.float32),
            pltpu.VMEM((8, COEFFS, COEFFS), jnp.bfloat16),
            pltpu.VMEM((8, GROUP // 8, COEFFS), jnp.bfloat16),
            pltpu.VMEM((2 * PARENTS, LANES), jnp.float32),
            pltpu.VMEM((2 * SLOTS, LANES), jnp.float32),
            pltpu.SemaphoreType.DMA((CHUNKS,)),
            pltpu.SemaphoreType.DMA(()),
        ],
        compiler_params=pltpu.CompilerParams(vmem_limit_bytes=60 << 20),
        cost_estimate=pl.CostEstimate(flops=10_000_000_000, bytes_accessed=8 << 20, transcendentals=0),
    )(picks, place, multipoles, m2m)


def translate(name, sources, which_core, weights, swapped, multipoles, parts, gflops):
    targets = sources.shape[1]
    tiles = targets // TILE
    n = len(parts)
    width = OPS * TILE // LANES
    src = sources.reshape(OPS, tiles, TILE).swapaxes(0, 1).reshape(tiles * width, LANES)
    leaves = [] if multipoles is None else [multipoles]
    starts = [2 * LEAVES * len(leaves)]
    for p in parts:
        starts.append(starts[-1] + p.shape[0])
    slots = starts[-1]

    def body(core, src_ref, *refs):
        here, mine, other = refs[0], refs[1:4], refs[4:7]
        refs = refs[7:]
        part_refs = refs[:n]
        refs = refs[n:]
        x_hbm = refs[: len(leaves)]
        refs = refs[len(leaves) :]
        out, buf, z, raw, w, wsem = refs[:6]
        loads = []
        if leaves:
            x, spread, xsem = refs[6:]
            loads = column_loads(x_hbm[0], x, xsem)
            for load in loads:
                load.start()

        pltpu.make_async_copy(here, raw.at[pl.ds(0, 4)], wsem.at[0]).start()
        for q in range(3):
            into = raw.at[pl.ds(4 * q + 4, 4)]

            @pl.when(core[0] != swapped)
            def _():
                pltpu.make_async_copy(mine[q], into, wsem.at[q + 1]).start()

            @pl.when(core[0] == swapped)
            def _():
                pltpu.make_async_copy(other[q], into, wsem.at[q + 1]).start()

        buf[pl.ds(slots, 2 * TAIL)] = jnp.zeros((2 * TAIL, LANES), jnp.float32)
        for k in range(n):
            buf[pl.ds(starts[k], starts[k + 1] - starts[k])] = part_refs[k][...].astype(jnp.float32)
        if leaves:
            spread[...] = spread_matrix()
            for k in range(CHUNKS):
                loads[k].wait()
                columns_to_rows(x, spread, buf, k)
        for q in range(4):
            pltpu.make_async_copy(here, raw.at[pl.ds(4 * q, 4)], wsem.at[q]).wait()
        r = lax.broadcasted_iota(jnp.int32, (2 * LANES, COEFFS), 0)
        c = lax.broadcasted_iota(jnp.int32, (2 * LANES, COEFFS), 1)
        unit = jnp.where(r == c, 1.0, 0.0).astype(jnp.bfloat16)
        for o in range(OPS):
            w[o * 2 * LANES : (o + 1) * 2 * LANES] = contract_lanes(unit, raw[o]).astype(jnp.bfloat16)

        @pl.loop(0, tiles)
        def _(tile):
            for o in range(OPS):
                for u in range(TILE):
                    f = o * TILE + u
                    slot = src_ref.at[:, pl.ds(f % LANES, 1)][tile * width + f // LANES, 0]
                    z[o, u] = buf[pl.ds(slot, 2), :]
            halves = []
            for o in range(OPS):
                box = z.at[o].reshape(2 * TILE, LANES)
                for h in range(2):
                    halves.append(box[pl.ds(h, TILE, 2), :].astype(jnp.bfloat16))
            total = jnp.dot(jnp.concatenate(halves, axis=1), w[...], preferred_element_type=jnp.float32)
            columns = pl.ds(pl.multiple_of(tile * TILE, TILE), TILE)
            out[:, columns] = total.T

    return pl.pallas_call(
        body,
        name=name,
        in_specs=[SMEM, SMEM] + [ANY] * 7 + [VMEM] * n + [ANY] * len(leaves),
        out_specs=VMEM,
        out_shape=jax.ShapeDtypeStruct((COEFFS, targets), jnp.float32),
        scratch_shapes=[
            pltpu.VMEM((slots + 2 * TAIL, LANES), jnp.float32),
            pltpu.VMEM((OPS, TILE, 2, LANES), jnp.float32),
            pltpu.VMEM((OPS, COEFFS, COEFFS), jnp.bfloat16),
            pltpu.VMEM((OPS * 2 * LANES, COEFFS), jnp.bfloat16),
            pltpu.SemaphoreType.DMA((4,)),
        ]
        + [
            pltpu.VMEM((COEFFS, LEAVES), jnp.bfloat16),
            pltpu.VMEM((2 * LANES, 2 * LANES), jnp.bfloat16),
            pltpu.SemaphoreType.DMA((CHUNKS,)),
        ]
        * len(leaves),
        compiler_params=pltpu.CompilerParams(vmem_limit_bytes=60 << 20),
        cost_estimate=pl.CostEstimate(flops=gflops * 1_000_000_000, bytes_accessed=10 << 20, transcendentals=0),
    )(which_core, src, *weights, *parts, *leaves)


def passed_along(block, axis, distance):
    devices = range(lax.axis_size(axis))
    route = [(i - distance, i) for i in devices if i - distance in devices]
    return lax.ppermute(block, axis, route)


def turned(block, distance):
    size = lax.axis_size("lvl")
    return lax.ppermute(block, "lvl", [((i + distance) % size, i) for i in range(size)])


def swapped_cores(block):
    return lax.ppermute(block, "slab", [(i ^ 1, i) for i in range(lax.axis_size("slab"))])


def sources_here(sources, level_here, level_count):
    quarter = sources.shape[1] // level_count
    here = 2 * lax.dynamic_slice_in_dim(sources, level_here * quarter, quarter, 1)
    return lax.dynamic_slice_in_dim(jnp.concatenate([here, here], axis=0), level_here * (OPS // level_count), OPS, 0)


def per_device(multipoles, fine_m2l, m2m, coarse_m2l, fine_source, ghost_index, ghost_count, owner, coarse_source):
    slab_count = lax.axis_size("slab")
    slab_here = lax.axis_index("slab")
    level_count = lax.axis_size("lvl")
    level_here = lax.axis_index("lvl")

    core = slab_here % 2
    fetched = jnp.where(core == 0, fine_m2l, coarse_m2l)
    mine = [turned(fetched, d) for d in (1, 2, 3)]
    other = [swapped_cores(m) for m in mine]
    core_flag = core.astype(jnp.int32).reshape(1)

    index_here = lax.dynamic_slice_in_dim(ghost_index, slab_here * GHOST, GHOST, 1)
    count_here = lax.dynamic_slice_in_dim(ghost_count, slab_here, 1, 1)
    inside = jnp.arange(GHOST, dtype=jnp.int32)[None, :] < count_here
    picks = jnp.where(inside, 2 * index_here, 2 * LEAVES).reshape(2 * GHOST // LANES, LANES)
    owners = owner[:, 0]
    matches = (owners[:, None] == jnp.arange(slab_count, dtype=jnp.int32)[None, :]).astype(jnp.bfloat16)
    order = jnp.arange(PARENTS, dtype=jnp.int32)
    earlier = (order[None, :] < order[:, None]).astype(jnp.bfloat16)
    before = jnp.dot(earlier, matches, preferred_element_type=jnp.float32)
    rank = jnp.sum(before * matches.astype(jnp.float32), axis=1).astype(jnp.int32)
    capacity = SLOTS // slab_count
    place = (2 * (owners * capacity + rank)).reshape(PARENTS // LANES, LANES)
    down, up, outgoing = upward(multipoles, m2m, picks, place)
    upper = passed_along(down, "slab", -1)
    lower = passed_along(up, "slab", 1)
    received = lax.all_to_all(
        outgoing.reshape(slab_count, 2 * capacity, LANES), "slab", split_axis=0, concat_axis=0, tiled=True
    ).reshape(2 * SLOTS, LANES)

    fine_local = translate(
        "fine",
        sources_here(fine_source, level_here, level_count),
        core_flag,
        [fine_m2l, *mine, *other],
        1,
        multipoles,
        [lower, upper],
        20,
    )
    coarse_local = translate(
        "coarse",
        sources_here(coarse_source, level_here, level_count),
        core_flag,
        [coarse_m2l, *mine, *other],
        0,
        None,
        [received],
        6,
    )
    return (fine_local, coarse_local)


def solution(mesh):
    placed = (
        P(None, "slab"),
        P("lvl", None, None),
        P(),
        P("lvl", None, None),
        P(None, "slab"),
        P(),
        P(),
        P("slab", None),
        P(None, "slab"),
    )
    return jax.shard_map(
        per_device,
        mesh=mesh,
        in_specs=placed,
        out_specs=(P(None, ("slab", "lvl")), P(None, ("slab", "lvl"))),
        check_vma=False,
    )
```
